32 devices in a mesh: ctx: 8 (over y, x, core), kv: 4 (over z).
Axes of the slice: x: 2, y: 2, z: 4, core: 2. Of those that a mesh axis runs over, the one named last changes fastest.
Arguments:
- queries: bfloat16 [3072, 64, 128], P('ctx', 'kv'), may hold values from -128 to 128
- key_heads: bfloat16 [3072, 8, 128], P('ctx', 'kv'), may hold values from -6 to 6
- value_heads: bfloat16 [3072, 8, 128], P('ctx', 'kv'), may hold values from -6 to 6
- grad_out: bfloat16 [3072, 64, 128], P('ctx', 'kv'), may hold values from -6 to 6
- transforms: float32 [8, 128, 128], P('ctx'), may hold values from -1.2 to 1.2
- window: int32 [8], P('kv'), may hold values from 1 to 4, as said below
- first_block: int32 [1], replicated, may hold values from 0 to 7
Outputs:
- query_grad: bfloat16 [3072, 64, 128], P('ctx', 'kv')
- key_grad: bfloat16 [3072, 8, 128], P('ctx', 'kv')
- value_grad: bfloat16 [3072, 8, 128], P('ctx', 'kv')
- turn_grad: float32 [8, 128, 128], P('ctx')
The draws below stay inside these ranges and needn't reach their ends.
Inputs may be any that keep to these rules, and one draw needn't show every extreme that they name: Some key-value head has a window of 4 blocks.
All inputs are finite; a program needn't handle non-finite values.
Results may differ from the reference program's by a relative error of at most 0.019.
Values may be sent and summed in bfloat16 or wider, within the bound.
A program may use at most 256 MiB of HBM per device.

```python
import math
import jax
import jax.numpy as jnp
from jax import lax

D = 128
HQ = 64
KVH = 8
TOK_DEV = 384
HOPS = 3
NBLK = 8
TOKENS = 3072


def drawn_keys(key):
    sample = jnp.clip(jax.random.normal(jax.random.fold_in(key, 11), (TOKENS, KVH, D), jnp.float32), -6.0, 6.0)
    return sample


def draw_key_heads(key, part):
    return drawn_keys(key).astype(jnp.bfloat16)


def draw_queries(key, part):
    sample = jnp.clip(jax.random.normal(jax.random.fold_in(key, 12), (TOKENS, HQ, D), jnp.float32), -6.0, 6.0)
    return sample.astype(jnp.bfloat16)


def draw_transforms(key, part):
    sample = jax.random.normal(jax.random.fold_in(key, 21), (NBLK, D, D), jnp.float32)
    orthogonal, triangle = jnp.linalg.qr(sample)
    gain_rows = jax.random.uniform(jax.random.fold_in(key, 22), (NBLK, 1, 1), jnp.float32, 0.85, 1.15)
    return orthogonal * gain_rows


def draw_window(key, part):
    sample = jax.random.randint(jax.random.fold_in(key, 31), (KVH,), 1, HOPS + 2)
    widest = jax.random.randint(jax.random.fold_in(key, 32), (), 0, KVH)
    return jnp.where(jnp.arange(KVH) == widest, HOPS + 1, sample).astype(jnp.int32)


def shard_levels(key, extent, cuts, low, top_value):
    gain, own = 1.0, jax.random.fold_in(key, 6)
    for dim, shards_of in cuts:
        heights = jnp.exp(jax.random.uniform(jax.random.fold_in(own, dim), (shards_of,), jnp.float32, low / len(cuts), top_value / len(cuts)))
        gain = gain * jnp.repeat(heights, extent[dim] // shards_of).reshape([-1 if axis == dim else 1 for axis in range(len(extent))])
    return gain


def scatter_about(stream_key, shape, deviation, bound, shards=(), kind=jnp.bfloat16):
    gain = shard_levels(stream_key, shape, shards, -0.22, 0.18) if shards else 1.0
    result = jax.random.normal(stream_key, shape, jnp.float32) * deviation * gain
    return jnp.minimum(jnp.maximum(result, -bound), bound).astype(kind)


def setup_inputs(seed: int = 0) -> dict:
    streams_of = jax.random.split(jax.random.key(seed), 8)
    queries = draw_queries(jax.random.fold_in(streams_of[7], 71), 0)
    key_heads = draw_key_heads(jax.random.fold_in(streams_of[7], 71), 0)
    value_heads = scatter_about(streams_of[2], (TOKENS, KVH, D), 1.0, 6.0, ((0, 8), (1, 4)))
    grad_out = scatter_about(streams_of[3], (TOKENS, HQ, D), 1.0, 6.0, ((0, 8), (1, 4)))
    transforms = draw_transforms(jax.random.fold_in(streams_of[7], 71), 0)
    window = draw_window(jax.random.fold_in(streams_of[7], 71), 0)
    first_block = jax.random.randint(streams_of[6], (1,), 0, NBLK).astype(jnp.int32)
    return {"queries": queries, "key_heads": key_heads, "value_heads": value_heads, "grad_out": grad_out, "transforms": transforms, "window": window, "first_block": first_block}


PRECISE = lax.Precision.HIGHEST

def halved(values_in):
    return lax.optimization_barrier(values_in.astype(jnp.bfloat16)).astype(jnp.float32)

def rotate_chain(keys_f, transforms):
    stacked = [keys_f]
    current = keys_f
    for hop_index in range(HOPS):
        turned = jnp.einsum('blgd,bed->blge', current, transforms, precision=PRECISE)
        current = jnp.roll(turned, 1, axis=0)
        stacked.append(current)
    return jnp.stack(stacked)

def reference(queries, key_heads, value_heads, grad_out, transforms, window, first_block):
    groups = HQ // KVH
    factor = 1.0 / math.sqrt(D)
    keys_f = key_heads.astype(jnp.float32).reshape(NBLK, TOK_DEV, KVH, D)
    visits = rotate_chain(keys_f, transforms)
    value_blocks = value_heads.reshape(NBLK, TOK_DEV, KVH, D)
    value_stack = jnp.stack([jnp.roll(value_blocks, hop_index, axis=0) for hop_index in range(HOPS + 1)])
    query_blocks = queries.reshape(NBLK, TOK_DEV, KVH, groups, D)
    grad_blocks = grad_out.reshape(NBLK, TOK_DEV, KVH, groups, D)
    position = (jnp.arange(NBLK).astype(jnp.int32) - first_block[0]) % NBLK
    hop_ids = jnp.arange(HOPS + 1).astype(jnp.int32)
    causal = jnp.arange(TOK_DEV)[:, None] >= jnp.arange(TOK_DEV)[None, :]
    causal_hops = (hop_ids[:, None, None] > 0) | causal[None]

    def one_block(block_index):
        query_f = query_blocks[block_index].astype(jnp.float32)
        grad_f = grad_blocks[block_index].astype(jnp.float32)
        key_tiles = halved(visits[:, block_index])
        value_f = value_stack[:, block_index].astype(jnp.float32)
        logits = jnp.einsum('lgjd,hmgd->hgjlm', query_f, key_tiles, precision=PRECISE) * factor
        usable = (hop_ids[:, None] < window[None, :]) & (position[block_index] - hop_ids >= 0)[:, None]
        keep_mask = usable[:, :, None, None, None] & causal_hops[:, None, None, :, :]
        logits = jnp.where(keep_mask, logits, -jnp.inf)
        row_max = lax.optimization_barrier(jnp.max(logits, axis=(0, 4)))
        row_total = lax.optimization_barrier(jnp.sum(jnp.exp(logits - row_max[None, :, :, :, None]), axis=(0, 4)))
        log_total = row_max + jnp.log(row_total)
        weights = jnp.exp(logits - log_total[None, :, :, :, None])
        slopes = jnp.einsum('lgjd,hmgd->hgjlm', grad_f, value_f, precision=PRECISE)
        row_dot = lax.optimization_barrier(jnp.sum(weights * slopes, axis=(0, 4)))
        score_half = halved(weights * (slopes - row_dot[None, :, :, :, None]))
        weight_half = halved(weights)
        query_grad = (jnp.einsum('hgjlm,hmgd->lgjd', score_half, key_tiles, precision=PRECISE) * factor).astype(jnp.bfloat16)
        tile_grad = jnp.einsum('hgjlm,lgjd->hmgd', score_half, query_f, precision=PRECISE) * factor
        value_part = jnp.einsum('hgjlm,lgjd->hmgd', weight_half, grad_f, precision=PRECISE)
        return (query_grad, tile_grad, value_part)
    query_grad, tile_grad, value_part = lax.map(one_block, jnp.arange(NBLK))
    rotated, pull = jax.vjp(rotate_chain, keys_f, transforms)
    key_grad, turn_grad = pull(jnp.swapaxes(tile_grad, 0, 1))
    value_grad = value_part[:, 0]
    for hop_index in range(1, HOPS + 1):
        value_grad = value_grad + jnp.roll(value_part[:, hop_index], -hop_index, axis=0)
    return (query_grad.reshape(TOKENS, HQ, D), key_grad.reshape(TOKENS, KVH, D).astype(jnp.bfloat16), value_grad.reshape(TOKENS, KVH, D).astype(jnp.bfloat16), turn_grad)
```

```python
import math

import jax
import jax.numpy as jnp
from jax import lax
from jax.experimental import pallas as pl
from jax.experimental.pallas import tpu as pltpu
from jax.sharding import PartitionSpec as P

HOPS = 3
CHUNK = 128
HALF = jnp.bfloat16
FULL = jnp.float32
PRECISE = lax.Precision.HIGHEST
NT = (((1,), (1,)), ((), ()))
TN = (((0,), (0,)), ((), ()))


def passed_along(shard, by):
    peers = lax.axis_size("ctx")
    return lax.ppermute(shard, "ctx", [(i, (i + by) % peers) for i in range(peers)])


def split_parts(matrix):
    upper = matrix.astype(HALF)
    lower = (matrix - upper.astype(FULL)).astype(HALF)
    return (upper, lower)


def times_split(rows_half, matrix, spec):
    upper, lower = split_parts(matrix)
    first = jnp.einsum(spec, rows_half, upper, preferred_element_type=FULL)
    return first + jnp.einsum(spec, rows_half, lower, preferred_element_type=FULL)


def attention_kernel(groups, factor, hops_ref, q_ref, g_ref, *refs):
    kv_refs = refs[: HOPS + 1]
    dq_ref, dk_ref, dv_ref, e_ref, slope_ref, max_ref, dk_acc, dv_acc, dq_acc = refs[HOPS + 1 :]
    tile = pl.program_id(0)
    tiles = pl.num_programs(0)
    rows = q_ref.shape[0]
    per_hop = kv_refs[0].shape[1] // CHUNK
    scale = factor * math.log2(math.e)
    hop_count = hops_ref[0]

    @pl.when(tile == 0)
    def _():
        dk_acc[...] = jnp.zeros_like(dk_acc)
        dv_acc[...] = jnp.zeros_like(dv_acc)

    def forward(keys, values, slot, state, masked):
        top, total, dot = state
        logits = lax.dot_general(keys, q_ref[...], NT, preferred_element_type=FULL) * scale
        if masked:
            key_at = lax.broadcasted_iota(jnp.int32, (CHUNK, rows), 0)
            row_at = lax.broadcasted_iota(jnp.int32, (CHUNK, rows), 1) // groups
            logits = jnp.where(key_at <= row_at, logits, -jnp.inf)
        slopes = lax.dot_general(values, g_ref[...], NT, preferred_element_type=FULL)
        chunk_max = jnp.max(logits, axis=0, keepdims=True)
        exps = jnp.exp2(logits - chunk_max)
        e_ref[slot] = exps
        slope_ref[slot] = slopes
        max_ref[slot] = chunk_max
        top_new = jnp.maximum(top, chunk_max)
        old, new = jnp.exp2(top - top_new), jnp.exp2(chunk_max - top_new)
        total = total * old + jnp.sum(exps, axis=0, keepdims=True) * new
        dot = dot * old + jnp.sum(exps * slopes, axis=0, keepdims=True) * new
        return top_new, total, dot

    def backward(keys, slot, state):
        top, inverse, dot = state
        part = jnp.exp2(max_ref[slot] - top) * inverse
        weights = e_ref[slot] * part
        scores = (weights * (slope_ref[slot] - dot)).astype(HALF)
        spot = pl.ds(pl.multiple_of(slot * CHUNK, CHUNK), CHUNK)
        dv_acc[spot, :] += jnp.dot(weights.astype(HALF), g_ref[...], preferred_element_type=FULL)
        dk_acc[spot, :] += jnp.dot(scores, q_ref[...], preferred_element_type=FULL)
        dq_acc[...] += lax.dot_general(keys, scores, TN, preferred_element_type=FULL)

    def spot_of(index):
        return pl.ds(pl.multiple_of(index * CHUNK, CHUNK), CHUNK)

    state = (
        jnp.full((1, rows), -jnp.inf, FULL),
        jnp.zeros((1, rows), FULL),
        jnp.zeros((1, rows), FULL),
    )
    own = kv_refs[0]
    state = forward(own[0, spot_of(tile), :], own[1, spot_of(tile), :], tile, state, True)
    state = lax.fori_loop(
        0,
        tile,
        lambda i, s: forward(own[0, spot_of(i), :], own[1, spot_of(i), :], i, s, False),
        state,
    )
    for hop in range(1, HOPS + 1):
        ref = kv_refs[hop]
        state = lax.fori_loop(
            0,
            jnp.where(hop < hop_count, per_hop, 0),
            lambda i, s, ref=ref, hop=hop: forward(
                ref[0, spot_of(i), :], ref[1, spot_of(i), :], hop * per_hop + i, s, False
            ),
            state,
        )
    top, total, dot = state
    inverse = 1.0 / total
    final = (top, inverse, dot * inverse)
    dq_acc[...] = jnp.zeros_like(dq_acc)
    for hop in range(HOPS + 1):
        ref = kv_refs[hop]
        trips = tile + 1 if hop == 0 else jnp.where(hop < hop_count, per_hop, 0)

        def step(i, carry, ref=ref, hop=hop):
            backward(ref[0, spot_of(i), :], hop * per_hop + i, final)
            return carry

        lax.fori_loop(0, trips, step, 0)
    dq_ref[...] = (dq_acc[...] * factor).T.astype(HALF)

    @pl.when(tile == tiles - 1)
    def _():
        dk_ref[...] = (dk_acc[...] * factor).astype(HALF)
        dv_ref[...] = dv_acc[...].astype(HALF)


def attention(hop_count, query_rows, grad_rows, pairs, groups, factor):
    total_rows, width = query_rows.shape
    length = pairs[0].shape[1]
    tiles = length // CHUNK
    rows = total_rows // tiles
    hops = len(pairs)
    keys = hops * length
    whole = lambda i: (0, 0, 0)
    row_spec = pl.BlockSpec((rows, width), lambda i: (i, 0))
    part_spec = pl.BlockSpec((keys, width), lambda i: (0, 0))
    chunks = keys // CHUNK
    return pl.pallas_call(
        lambda *refs: attention_kernel(groups, factor, *refs),
        grid=(tiles,),
        in_specs=[pl.BlockSpec(memory_space=pltpu.SMEM), row_spec, row_spec]
        + [pl.BlockSpec((2, length, width), whole)] * hops,
        out_specs=[row_spec, part_spec, part_spec],
        out_shape=[
            jax.ShapeDtypeStruct((total_rows, width), HALF),
            jax.ShapeDtypeStruct((keys, width), HALF),
            jax.ShapeDtypeStruct((keys, width), HALF),
        ],
        scratch_shapes=[
            pltpu.VMEM((chunks, CHUNK, rows), FULL),
            pltpu.VMEM((chunks, CHUNK, rows), FULL),
            pltpu.VMEM((chunks, 1, rows), FULL),
            pltpu.VMEM((keys, width), FULL),
            pltpu.VMEM((keys, width), FULL),
            pltpu.VMEM((width, rows), FULL),
        ],
        compiler_params=pltpu.CompilerParams(vmem_limit_bytes=40 * 1024 * 1024),
        cost_estimate=pl.CostEstimate(
            flops=10 * total_rows * keys * width,
            bytes_accessed=6 * total_rows * width + 8 * keys * width,
            transcendentals=total_rows * keys,
        ),
    )(hop_count, query_rows, grad_rows, *pairs)


def shards(queries, key_heads, value_heads, grad_out, transforms, window, first_block):
    length, head_count, width = queries.shape
    kv_heads = key_heads.shape[1]
    groups = head_count // kv_heads
    factor = 1.0 / math.sqrt(width)
    blocks = lax.axis_size("ctx")
    position = (lax.axis_index("ctx") - first_block[0]) % blocks
    hop_counts = jnp.minimum(window, position + 1)
    turns = [transforms[0]] + [passed_along(transforms[0], -h) for h in range(1, HOPS)]
    chain = [turns[0]]
    for h in range(1, HOPS):
        chain.append(jnp.dot(turns[h], chain[-1], precision=PRECISE))
    own_keys = key_heads.transpose(1, 0, 2)
    own_values = value_heads.transpose(1, 0, 2)
    query_rows = queries.reshape(length, kv_heads, groups, width).transpose(1, 0, 2, 3)
    grad_rows = grad_out.reshape(length, kv_heads, groups, width).transpose(1, 0, 2, 3)
    query_rows = query_rows.reshape(kv_heads, length * groups, width)
    grad_rows = grad_rows.reshape(kv_heads, length * groups, width)
    turned = [own_keys] + [times_split(own_keys, m, "gld,ed->gle").astype(HALF) for m in chain]
    query_parts, key_grads, value_grads = [], [], []
    turn_terms = [jnp.zeros((width, width), FULL) for _ in range(HOPS)]
    for g in range(kv_heads):
        pairs = [jnp.stack([own_keys[g], own_values[g]])]
        for h in range(1, HOPS + 1):
            pairs.append(passed_along(jnp.stack([turned[h][g], own_values[g]]), h))
        dq, dk, dv = attention(
            hop_counts[g : g + 1], query_rows[g], grad_rows[g], pairs, groups, factor
        )
        query_parts.append(dq)
        back = jnp.stack([dk, dv]).reshape(2, HOPS + 1, length, width)
        backs = [back[:, 0]] + [passed_along(back[:, h], -h) for h in range(1, HOPS + 1)]
        carried = backs[HOPS][0].astype(FULL)
        for h in range(HOPS, 0, -1):
            half = carried.astype(HALF)
            turn_terms[h - 1] += lax.dot_general(
                half, turned[h - 1][g], TN, preferred_element_type=FULL
            )
            carried = backs[h - 1][0].astype(FULL) + times_split(half, turns[h - 1], "le,ed->ld")
        key_grads.append(carried.astype(HALF))
        value_grads.append(sum(b[1].astype(FULL) for b in backs).astype(HALF))
    turn_total = turn_terms[0]
    for h in range(1, HOPS):
        turn_total = turn_total + passed_along(turn_terms[h].astype(HALF), h).astype(FULL)
    turn_total = lax.psum(turn_total.astype(HALF), "kv").astype(FULL)
    query_grad = jnp.stack(query_parts).reshape(kv_heads, length, groups, width)
    query_grad = query_grad.transpose(1, 0, 2, 3).reshape(length, head_count, width)
    return (
        query_grad,
        jnp.stack(key_grads, axis=1),
        jnp.stack(value_grads, axis=1),
        turn_total[None],
    )


def solution(mesh):
    return jax.shard_map(
        shards,
        mesh=mesh,
        in_specs=(
            P("ctx", "kv", None),
            P("ctx", "kv", None),
            P("ctx", "kv", None),
            P("ctx", "kv", None),
            P("ctx", None, None),
            P("kv"),
            P(),
        ),
        out_specs=(
            P("ctx", "kv", None),
            P("ctx", "kv", None),
            P("ctx", "kv", None),
            P("ctx", None, None),
        ),
        check_vma=False,
    )
```

```python
import math

import jax
import jax.numpy as jnp
from jax import lax
from jax.experimental import pallas as pl
from jax.experimental.pallas import tpu as pltpu
from jax.sharding import PartitionSpec as P

HOPS = 3
CHUNK = 128
HALF = jnp.bfloat16
FULL = jnp.float32
PRECISE = lax.Precision.HIGHEST
NT = (((1,), (1,)), ((), ()))
TN = (((0,), (0,)), ((), ()))


def passed_along(shard, by):
    peers = lax.axis_size("ctx")
    return lax.ppermute(shard, "ctx", [(i, (i + by) % peers) for i in range(peers)])


def split_parts(matrix):
    upper = matrix.astype(HALF)
    lower = (matrix - upper.astype(FULL)).astype(HALF)
    return (upper, lower)


def times_split(rows_half, matrix, spec):
    upper, lower = split_parts(matrix)
    first = jnp.einsum(spec, rows_half, upper, preferred_element_type=FULL)
    return first + jnp.einsum(spec, rows_half, lower, preferred_element_type=FULL)


def attention_kernel(groups, factor, hops_ref, turn_ref, q_ref, g_ref, *refs):
    kv_refs = refs[: HOPS + 1]
    dq_ref, dk_ref, dv_ref, e_ref, slope_ref, max_ref, dk_acc, dv_acc, dq_acc, tile_ref = (
        refs[HOPS + 1 :]
    )
    tile = pl.program_id(0)
    tiles = pl.num_programs(0)
    rows = q_ref.shape[0]
    per_hop = kv_refs[0].shape[1] // CHUNK
    scale = factor * math.log2(math.e)
    hop_count = hops_ref[0]

    @pl.when(tile == 0)
    def _():
        dk_acc[...] = jnp.zeros_like(dk_acc)
        dv_acc[...] = jnp.zeros_like(dv_acc)
        tile_ref[0] = kv_refs[0][0]
        for hop in range(1, HOPS + 1):
            keys = kv_refs[hop][0]
            first = lax.dot_general(keys, turn_ref[hop - 1, 0], NT, preferred_element_type=FULL)
            second = lax.dot_general(keys, turn_ref[hop - 1, 1], NT, preferred_element_type=FULL)
            tile_ref[hop] = (first + second).astype(HALF)

    def forward(keys, values, slot, state, masked):
        top, total, dot = state
        logits = lax.dot_general(keys, q_ref[...], NT, preferred_element_type=FULL) * scale
        if masked:
            key_at = lax.broadcasted_iota(jnp.int32, (CHUNK, rows), 0)
            row_at = lax.broadcasted_iota(jnp.int32, (CHUNK, rows), 1) // groups
            logits = jnp.where(key_at <= row_at, logits, -jnp.inf)
        slopes = lax.dot_general(values, g_ref[...], NT, preferred_element_type=FULL)
        chunk_max = jnp.max(logits, axis=0, keepdims=True)
        exps = jnp.exp2(logits - chunk_max)
        e_ref[slot] = exps
        slope_ref[slot] = slopes
        max_ref[slot] = chunk_max
        top_new = jnp.maximum(top, chunk_max)
        old, new = jnp.exp2(top - top_new), jnp.exp2(chunk_max - top_new)
        total = total * old + jnp.sum(exps, axis=0, keepdims=True) * new
        dot = dot * old + jnp.sum(exps * slopes, axis=0, keepdims=True) * new
        return top_new, total, dot

    def backward(keys, slot, state):
        top, inverse, dot = state
        part = jnp.exp2(max_ref[slot] - top) * inverse
        weights = e_ref[slot] * part
        scores = (weights * (slope_ref[slot] - dot)).astype(HALF)
        spot = pl.ds(pl.multiple_of(slot * CHUNK, CHUNK), CHUNK)
        dv_acc[spot, :] += jnp.dot(weights.astype(HALF), g_ref[...], preferred_element_type=FULL)
        dk_acc[spot, :] += jnp.dot(scores, q_ref[...], preferred_element_type=FULL)
        dq_acc[...] += lax.dot_general(keys, scores, TN, preferred_element_type=FULL)

    def spot_of(index):
        return pl.ds(pl.multiple_of(index * CHUNK, CHUNK), CHUNK)

    state = (
        jnp.full((1, rows), -jnp.inf, FULL),
        jnp.zeros((1, rows), FULL),
        jnp.zeros((1, rows), FULL),
    )
    own = kv_refs[0]
    state = forward(tile_ref[0, spot_of(tile), :], own[1, spot_of(tile), :], tile, state, True)
    state = lax.fori_loop(
        0,
        tile,
        lambda i, s: forward(tile_ref[0, spot_of(i), :], own[1, spot_of(i), :], i, s, False),
        state,
    )
    for hop in range(1, HOPS + 1):
        ref = kv_refs[hop]
        state = lax.fori_loop(
            0,
            jnp.where(hop < hop_count, per_hop, 0),
            lambda i, s, ref=ref, hop=hop: forward(
                tile_ref[hop, spot_of(i), :],
                ref[1, spot_of(i), :],
                hop * per_hop + i,
                s,
                False,
            ),
            state,
        )
    top, total, dot = state
    inverse = 1.0 / total
    final = (top, inverse, dot * inverse)
    dq_acc[...] = jnp.zeros_like(dq_acc)
    for hop in range(HOPS + 1):
        trips = tile + 1 if hop == 0 else jnp.where(hop < hop_count, per_hop, 0)

        def step(i, carry, hop=hop):
            backward(tile_ref[hop, spot_of(i), :], hop * per_hop + i, final)
            return carry

        lax.fori_loop(0, trips, step, 0)
    dq_ref[...] = (dq_acc[...] * factor).T.astype(HALF)

    @pl.when(tile == tiles - 1)
    def _():
        dk_ref[...] = (dk_acc[...] * factor).astype(HALF)
        dv_ref[...] = dv_acc[...].astype(HALF)


def attention(hop_count, turn_parts, query_rows, grad_rows, pairs, groups, factor):
    total_rows, width = query_rows.shape
    length = pairs[0].shape[1]
    tiles = length // CHUNK
    rows = total_rows // tiles
    hops = len(pairs)
    keys = hops * length
    whole = lambda i: (0, 0, 0)
    row_spec = pl.BlockSpec((rows, width), lambda i: (i, 0))
    part_spec = pl.BlockSpec((keys, width), lambda i: (0, 0))
    chunks = keys // CHUNK
    return pl.pallas_call(
        lambda *refs: attention_kernel(groups, factor, *refs),
        grid=(tiles,),
        in_specs=[
            pl.BlockSpec(memory_space=pltpu.SMEM),
            pl.BlockSpec(turn_parts.shape, lambda i: (0, 0, 0, 0)),
            row_spec,
            row_spec,
        ]
        + [pl.BlockSpec((2, length, width), whole)] * hops,
        out_specs=[row_spec, part_spec, part_spec],
        out_shape=[
            jax.ShapeDtypeStruct((total_rows, width), HALF),
            jax.ShapeDtypeStruct((keys, width), HALF),
            jax.ShapeDtypeStruct((keys, width), HALF),
        ],
        scratch_shapes=[
            pltpu.VMEM((chunks, CHUNK, rows), FULL),
            pltpu.VMEM((chunks, CHUNK, rows), FULL),
            pltpu.VMEM((chunks, 1, rows), FULL),
            pltpu.VMEM((keys, width), FULL),
            pltpu.VMEM((keys, width), FULL),
            pltpu.VMEM((width, rows), FULL),
            pltpu.VMEM((hops, length, width), HALF),
        ],
        compiler_params=pltpu.CompilerParams(vmem_limit_bytes=40 * 1024 * 1024),
        cost_estimate=pl.CostEstimate(
            flops=10 * total_rows * keys * width,
            bytes_accessed=6 * total_rows * width + 8 * keys * width,
            transcendentals=total_rows * keys,
        ),
    )(hop_count, turn_parts, query_rows, grad_rows, *pairs)


def shards(queries, key_heads, value_heads, grad_out, transforms, window, first_block):
    length, head_count, width = queries.shape
    kv_heads = key_heads.shape[1]
    groups = head_count // kv_heads
    factor = 1.0 / math.sqrt(width)
    blocks = lax.axis_size("ctx")
    position = (lax.axis_index("ctx") - first_block[0]) % blocks
    hop_counts = jnp.minimum(window, position + 1)
    pairs = [
        [jnp.stack([key_heads[:, g], value_heads[:, g]])] for g in range(kv_heads)
    ]
    arriving = [passed_along(transforms[0], h) for h in range(1, HOPS + 1)]
    for g in range(kv_heads):
        for h in range(1, HOPS + 1):
            pairs[g].append(passed_along(pairs[g][0], h))
    met = [arriving[0]]
    for h in range(1, HOPS):
        met.append(jnp.dot(met[-1], arriving[h], precision=PRECISE))
    turn_parts = jnp.stack([jnp.stack(split_parts(m)) for m in met])
    turns = [transforms[0]] + [passed_along(transforms[0], -h) for h in range(1, HOPS)]
    chain = [turns[0]]
    for h in range(1, HOPS - 1):
        chain.append(jnp.dot(turns[h], chain[-1], precision=PRECISE))
    own_keys = key_heads.transpose(1, 0, 2)
    query_rows = queries.reshape(length, kv_heads, groups, width).transpose(1, 0, 2, 3)
    grad_rows = grad_out.reshape(length, kv_heads, groups, width).transpose(1, 0, 2, 3)
    query_rows = query_rows.reshape(kv_heads, length * groups, width)
    grad_rows = grad_rows.reshape(kv_heads, length * groups, width)
    turned = [own_keys] + [times_split(own_keys, m, "gld,ed->gle").astype(HALF) for m in chain]
    query_parts, key_grads, value_grads = [], [], []
    turn_terms = [jnp.zeros((width, width), FULL) for _ in range(HOPS)]
    for g in range(kv_heads):
        dq, dk, dv = attention(
            hop_counts[g : g + 1],
            turn_parts,
            query_rows[g],
            grad_rows[g],
            pairs[g],
            groups,
            factor,
        )
        query_parts.append(dq)
        back = jnp.stack([dk, dv]).reshape(2, HOPS + 1, length, width)
        backs = [back[:, 0]] + [passed_along(back[:, h], -h) for h in range(1, HOPS + 1)]
        carried = backs[HOPS][0].astype(FULL)
        for h in range(HOPS, 0, -1):
            half = carried.astype(HALF)
            turn_terms[h - 1] += lax.dot_general(
                half, turned[h - 1][g], TN, preferred_element_type=FULL
            )
            carried = backs[h - 1][0].astype(FULL) + times_split(half, turns[h - 1], "le,ed->ld")
        key_grads.append(carried.astype(HALF))
        value_grads.append(sum(b[1].astype(FULL) for b in backs).astype(HALF))
    turn_total = turn_terms[0]
    for h in range(1, HOPS):
        turn_total = turn_total + passed_along(turn_terms[h].astype(HALF), h).astype(FULL)
    turn_total = lax.psum(turn_total.astype(HALF), "kv").astype(FULL)
    query_grad = jnp.stack(query_parts).reshape(kv_heads, length, groups, width)
    query_grad = query_grad.transpose(1, 0, 2, 3).reshape(length, head_count, width)
    return (
        query_grad,
        jnp.stack(key_grads, axis=1),
        jnp.stack(value_grads, axis=1),
        turn_total[None],
    )


def solution(mesh):
    return jax.shard_map(
        shards,
        mesh=mesh,
        in_specs=(
            P("ctx", "kv", None),
            P("ctx", "kv", None),
            P("ctx", "kv", None),
            P("ctx", "kv", None),
            P("ctx", None, None),
            P("kv"),
            P(),
        ),
        out_specs=(
            P("ctx", "kv", None),
            P("ctx", "kv", None),
            P("ctx", "kv", None),
            P("ctx", None, None),
        ),
        check_vma=False,
    )
```

```python
import math

import jax
import jax.numpy as jnp
from jax import lax
from jax.experimental import pallas as pl
from jax.experimental.pallas import tpu as pltpu
from jax.sharding import PartitionSpec as P

HOPS = 3
CHUNK = 128
HALF = jnp.bfloat16
FULL = jnp.float32
PRECISE = lax.Precision.HIGHEST
NT = (((1,), (1,)), ((), ()))
TN = (((0,), (0,)), ((), ()))


def passed_along(shard, by):
    peers = lax.axis_size("ctx")
    return lax.ppermute(shard, "ctx", [(i, (i + by) % peers) for i in range(peers)])


def split_parts(matrix):
    upper = matrix.astype(HALF)
    lower = (matrix - upper.astype(FULL)).astype(HALF)
    return (upper, lower)


def times_split(rows_half, matrix, spec):
    upper, lower = split_parts(matrix)
    first = jnp.einsum(spec, rows_half, upper, preferred_element_type=FULL)
    return first + jnp.einsum(spec, rows_half, lower, preferred_element_type=FULL)


def attention_kernel(groups, factor, hops_ref, turn_ref, q_ref, g_ref, *refs):
    kv_refs = refs[: HOPS + 1]
    dq_ref, dk_ref, dv_ref, e_ref, slope_ref, max_ref, dk_acc, dv_acc, dq_acc, tile_ref = (
        refs[HOPS + 1 :]
    )
    tile = pl.program_id(0)
    tiles = pl.num_programs(0)
    rows = q_ref.shape[0]
    per_hop = kv_refs[0].shape[1] // CHUNK
    scale = factor * math.log2(math.e)
    hop_count = hops_ref[0]

    @pl.when(tile == 0)
    def _():
        dk_acc[...] = jnp.zeros_like(dk_acc)
        dv_acc[...] = jnp.zeros_like(dv_acc)
        tile_ref[0] = kv_refs[0][0]
        for hop in range(1, HOPS + 1):
            keys = kv_refs[hop][0]
            first = lax.dot_general(keys, turn_ref[hop - 1, 0], NT, preferred_element_type=FULL)
            second = lax.dot_general(keys, turn_ref[hop - 1, 1], NT, preferred_element_type=FULL)
            tile_ref[hop] = (first + second).astype(HALF)

    def forward(keys, values, slot, state, masked):
        top, total, dot = state
        logits = lax.dot_general(keys, q_ref[...], NT, preferred_element_type=FULL) * scale
        if masked:
            key_at = lax.broadcasted_iota(jnp.int32, (CHUNK, rows), 0)
            row_at = lax.broadcasted_iota(jnp.int32, (CHUNK, rows), 1) // groups
            logits = jnp.where(key_at <= row_at, logits, -jnp.inf)
        slopes = lax.dot_general(values, g_ref[...], NT, preferred_element_type=FULL)
        chunk_max = jnp.max(logits, axis=0, keepdims=True)
        exps = jnp.exp2(logits - chunk_max)
        e_ref[slot] = exps
        slope_ref[slot] = slopes
        max_ref[slot] = chunk_max
        top_new = jnp.maximum(top, chunk_max)
        old, new = jnp.exp2(top - top_new), jnp.exp2(chunk_max - top_new)
        total = total * old + jnp.sum(exps, axis=0, keepdims=True) * new
        dot = dot * old + jnp.sum(exps * slopes, axis=0, keepdims=True) * new
        return top_new, total, dot

    def backward(keys, slot, state):
        top, inverse, dot = state
        part = jnp.exp2(max_ref[slot] - top) * inverse
        weights = e_ref[slot] * part
        scores = (weights * (slope_ref[slot] - dot)).astype(HALF)
        spot = pl.ds(pl.multiple_of(slot * CHUNK, CHUNK), CHUNK)
        dv_acc[spot, :] += jnp.dot(weights.astype(HALF), g_ref[...], preferred_element_type=FULL)
        dk_acc[spot, :] += jnp.dot(scores, q_ref[...], preferred_element_type=FULL)
        dq_acc[...] += lax.dot_general(keys, scores, TN, preferred_element_type=FULL)

    def spot_of(index):
        return pl.ds(pl.multiple_of(index * CHUNK, CHUNK), CHUNK)

    state = (
        jnp.full((1, rows), -jnp.inf, FULL),
        jnp.zeros((1, rows), FULL),
        jnp.zeros((1, rows), FULL),
    )
    own = kv_refs[0]
    state = forward(tile_ref[0, spot_of(tile), :], own[1, spot_of(tile), :], tile, state, True)
    state = lax.fori_loop(
        0,
        tile,
        lambda i, s: forward(tile_ref[0, spot_of(i), :], own[1, spot_of(i), :], i, s, False),
        state,
    )
    for hop in range(1, HOPS + 1):
        ref = kv_refs[hop]
        state = lax.fori_loop(
            0,
            jnp.where(hop < hop_count, per_hop, 0),
            lambda i, s, ref=ref, hop=hop: forward(
                tile_ref[hop, spot_of(i), :],
                ref[1, spot_of(i), :],
                hop * per_hop + i,
                s,
                False,
            ),
            state,
        )
    top, total, dot = state
    inverse = 1.0 / total
    final = (top, inverse, dot * inverse)
    dq_acc[...] = jnp.zeros_like(dq_acc)
    for hop in range(HOPS + 1):
        trips = tile + 1 if hop == 0 else jnp.where(hop < hop_count, per_hop, 0)

        def step(i, carry, hop=hop):
            backward(tile_ref[hop, spot_of(i), :], hop * per_hop + i, final)
            return carry

        lax.fori_loop(0, trips, step, 0)
    dq_ref[...] = (dq_acc[...] * factor).T.astype(HALF)

    @pl.when(tile == tiles - 1)
    def _():
        dk_ref[...] = (dk_acc[...] * factor).astype(HALF)
        dv_ref[...] = dv_acc[...].astype(HALF)


def attention(hop_count, turn_parts, query_rows, grad_rows, pairs, groups, factor):
    total_rows, width = query_rows.shape
    length = pairs[0].shape[1]
    tiles = length // CHUNK
    rows = total_rows // tiles
    hops = len(pairs)
    keys = hops * length
    whole = lambda i: (0, 0, 0)
    row_spec = pl.BlockSpec((rows, width), lambda i: (i, 0))
    part_spec = pl.BlockSpec((keys, width), lambda i: (0, 0))
    chunks = keys // CHUNK
    return pl.pallas_call(
        lambda *refs: attention_kernel(groups, factor, *refs),
        grid=(tiles,),
        in_specs=[
            pl.BlockSpec(memory_space=pltpu.SMEM),
            pl.BlockSpec(turn_parts.shape, lambda i: (0, 0, 0, 0)),
            row_spec,
            row_spec,
        ]
        + [pl.BlockSpec((2, length, width), whole)] * hops,
        out_specs=[row_spec, part_spec, part_spec],
        out_shape=[
            jax.ShapeDtypeStruct((total_rows, width), HALF),
            jax.ShapeDtypeStruct((keys, width), HALF),
            jax.ShapeDtypeStruct((keys, width), HALF),
        ],
        scratch_shapes=[
            pltpu.VMEM((chunks, CHUNK, rows), FULL),
            pltpu.VMEM((chunks, CHUNK, rows), FULL),
            pltpu.VMEM((chunks, 1, rows), FULL),
            pltpu.VMEM((keys, width), FULL),
            pltpu.VMEM((keys, width), FULL),
            pltpu.VMEM((width, rows), FULL),
            pltpu.VMEM((hops, length, width), HALF),
        ],
        compiler_params=pltpu.CompilerParams(vmem_limit_bytes=40 * 1024 * 1024),
        cost_estimate=pl.CostEstimate(
            flops=10 * total_rows * keys * width,
            bytes_accessed=6 * total_rows * width + 8 * keys * width,
            transcendentals=total_rows * keys,
        ),
    )(hop_count, turn_parts, query_rows, grad_rows, *pairs)


def turn_sum_kernel(blocks, peers, terms_ref, out_ref, slots, send_sem, recv_sem):
    me, lane = lax.axis_index("ctx"), lax.axis_index("kv")
    pairs = [(j, z) for j in range(HOPS) for z in range(peers) if j or z]
    barrier = pltpu.get_barrier_semaphore()
    for j, z in pairs:
        source = (lax.rem(me - j + blocks, blocks), lax.rem(lane - z + peers, peers))
        pl.semaphore_signal(
            barrier, inc=1, device_id=source, device_id_type=pl.DeviceIdType.MESH
        )
    pl.semaphore_wait(barrier, len(pairs))
    copies = []
    for k, (j, z) in enumerate(pairs):
        copy = pltpu.make_async_remote_copy(
            src_ref=terms_ref.at[j],
            dst_ref=slots.at[k],
            send_sem=send_sem.at[k],
            recv_sem=recv_sem.at[k],
            device_id=(lax.rem(me + j, blocks), lax.rem(lane + z, peers)),
            device_id_type=pl.DeviceIdType.MESH,
        )
        copy.start()
        copies.append(copy)
    total = terms_ref[0].astype(FULL)
    for k, copy in enumerate(copies):
        copy.wait_recv()
        total = total + slots[k].astype(FULL)
    out_ref[...] = total
    for copy in copies:
        copy.wait_send()


def turn_sum(terms):
    blocks, peers = lax.axis_size("ctx"), lax.axis_size("kv")
    count = HOPS * peers - 1
    return pl.pallas_call(
        lambda *refs: turn_sum_kernel(blocks, peers, *refs),
        out_shape=jax.ShapeDtypeStruct(terms.shape[1:], FULL),
        in_specs=[pl.BlockSpec(memory_space=pltpu.VMEM)],
        out_specs=pl.BlockSpec(memory_space=pltpu.VMEM),
        scratch_shapes=[
            pltpu.VMEM((count,) + terms.shape[1:], HALF),
            pltpu.SemaphoreType.DMA((count,)),
            pltpu.SemaphoreType.DMA((count,)),
        ],
        compiler_params=pltpu.CompilerParams(collective_id=0, has_side_effects=True),
    )(terms)


def shards(queries, key_heads, value_heads, grad_out, transforms, window, first_block):
    length, head_count, width = queries.shape
    kv_heads = key_heads.shape[1]
    groups = head_count // kv_heads
    factor = 1.0 / math.sqrt(width)
    blocks = lax.axis_size("ctx")
    position = (lax.axis_index("ctx") - first_block[0]) % blocks
    hop_counts = jnp.minimum(window, position + 1)
    pairs = [
        [jnp.stack([key_heads[:, g], value_heads[:, g]])] for g in range(kv_heads)
    ]
    arriving = [passed_along(transforms[0], h) for h in range(1, HOPS + 1)]
    for g in range(kv_heads):
        for h in range(1, HOPS + 1):
            pairs[g].append(passed_along(pairs[g][0], h))
    met = [arriving[0]]
    for h in range(1, HOPS):
        met.append(jnp.dot(met[-1], arriving[h], precision=PRECISE))
    turn_parts = jnp.stack([jnp.stack(split_parts(m)) for m in met])
    turns = [transforms[0]] + [passed_along(transforms[0], -h) for h in range(1, HOPS)]
    chain = [turns[0]]
    for h in range(1, HOPS - 1):
        chain.append(jnp.dot(turns[h], chain[-1], precision=PRECISE))
    own_keys = key_heads.transpose(1, 0, 2)
    query_rows = queries.reshape(length, kv_heads, groups, width).transpose(1, 0, 2, 3)
    grad_rows = grad_out.reshape(length, kv_heads, groups, width).transpose(1, 0, 2, 3)
    query_rows = query_rows.reshape(kv_heads, length * groups, width)
    grad_rows = grad_rows.reshape(kv_heads, length * groups, width)
    turned = [own_keys] + [times_split(own_keys, m, "gld,ed->gle").astype(HALF) for m in chain]
    query_parts, key_grads, value_grads = [], [], []
    turn_terms = [jnp.zeros((width, width), FULL) for _ in range(HOPS)]
    for g in range(kv_heads):
        dq, dk, dv = attention(
            hop_counts[g : g + 1],
            turn_parts,
            query_rows[g],
            grad_rows[g],
            pairs[g],
            groups,
            factor,
        )
        query_parts.append(dq)
        back = jnp.stack([dk, dv]).reshape(2, HOPS + 1, length, width)
        backs = [back[:, 0]] + [passed_along(back[:, h], -h) for h in range(1, HOPS + 1)]
        carried = backs[HOPS][0].astype(FULL)
        for h in range(HOPS, 0, -1):
            half = carried.astype(HALF)
            turn_terms[h - 1] += lax.dot_general(
                half, turned[h - 1][g], TN, preferred_element_type=FULL
            )
            carried = backs[h - 1][0].astype(FULL) + times_split(half, turns[h - 1], "le,ed->ld")
        key_grads.append(carried.astype(HALF))
        value_grads.append(sum(b[1].astype(FULL) for b in backs).astype(HALF))
    turn_total = turn_sum(jnp.stack(turn_terms).astype(HALF))
    query_grad = jnp.stack(query_parts).reshape(kv_heads, length, groups, width)
    query_grad = query_grad.transpose(1, 0, 2, 3).reshape(length, head_count, width)
    return (
        query_grad,
        jnp.stack(key_grads, axis=1),
        jnp.stack(value_grads, axis=1),
        turn_total[None],
    )


def solution(mesh):
    return jax.shard_map(
        shards,
        mesh=mesh,
        in_specs=(
            P("ctx", "kv", None),
            P("ctx", "kv", None),
            P("ctx", "kv", None),
            P("ctx", "kv", None),
            P("ctx", None, None),
            P("kv"),
            P(),
        ),
        out_specs=(
            P("ctx", "kv", None),
            P("ctx", "kv", None),
            P("ctx", "kv", None),
            P("ctx", None, None),
        ),
        check_vma=False,
    )
```

```python
import math

import jax
import jax.numpy as jnp
from jax import lax
from jax.experimental import pallas as pl
from jax.experimental.pallas import tpu as pltpu
from jax.sharding import PartitionSpec as P

HOPS = 3
CHUNK = 128
HALF = jnp.bfloat16
FULL = jnp.float32
PRECISE = lax.Precision.HIGHEST
NT = (((1,), (1,)), ((), ()))
TN = (((0,), (0,)), ((), ()))


def passed_along(shard, by):
    peers = lax.axis_size("ctx")
    return lax.ppermute(shard, "ctx", [(i, (i + by) % peers) for i in range(peers)])


def split_parts(matrix):
    upper = matrix.astype(HALF)
    lower = (matrix - upper.astype(FULL)).astype(HALF)
    return (upper, lower)


def times_split(rows_half, matrix, spec):
    upper, lower = split_parts(matrix)
    first = jnp.einsum(spec, rows_half, upper, preferred_element_type=FULL)
    return first + jnp.einsum(spec, rows_half, lower, preferred_element_type=FULL)


def attention_kernel(groups, factor, hops_ref, turn_ref, q_ref, g_ref, *refs):
    kv_refs = refs[: HOPS + 1]
    dq_ref, dk_ref, dv_ref, e_ref, slope_ref, max_ref, dk_acc, dv_acc, dq_acc, tile_ref = (
        refs[HOPS + 1 :]
    )
    tile = pl.program_id(0)
    tiles = pl.num_programs(0)
    rows = q_ref.shape[0]
    per_hop = kv_refs[0].shape[1] // CHUNK
    scale = factor * math.log2(math.e)
    hop_count = hops_ref[0]

    @pl.when(tile == 0)
    def _():
        dk_acc[...] = jnp.zeros_like(dk_acc)
        dv_acc[...] = jnp.zeros_like(dv_acc)
        tile_ref[0] = kv_refs[0][0]
        for hop in range(1, HOPS + 1):
            keys = kv_refs[hop][0]
            first = lax.dot_general(keys, turn_ref[hop - 1, 0], NT, preferred_element_type=FULL)
            second = lax.dot_general(keys, turn_ref[hop - 1, 1], NT, preferred_element_type=FULL)
            tile_ref[hop] = (first + second).astype(HALF)

    def forward(keys, values, slot, state, masked):
        top, total, dot = state
        logits = lax.dot_general(keys, q_ref[...], NT, preferred_element_type=FULL) * scale
        if masked:
            key_at = lax.broadcasted_iota(jnp.int32, (CHUNK, rows), 0)
            row_at = lax.broadcasted_iota(jnp.int32, (CHUNK, rows), 1) // groups
            logits = jnp.where(key_at <= row_at, logits, -jnp.inf)
        slopes = lax.dot_general(values, g_ref[...], NT, preferred_element_type=FULL)
        chunk_max = jnp.max(logits, axis=0, keepdims=True)
        exps = jnp.exp2(logits - chunk_max)
        e_ref[slot] = exps
        slope_ref[slot] = slopes
        max_ref[slot] = chunk_max
        top_new = jnp.maximum(top, chunk_max)
        old, new = jnp.exp2(top - top_new), jnp.exp2(chunk_max - top_new)
        total = total * old + jnp.sum(exps, axis=0, keepdims=True) * new
        dot = dot * old + jnp.sum(exps * slopes, axis=0, keepdims=True) * new
        return top_new, total, dot

    def backward(keys, slot, state):
        top, inverse, dot = state
        part = jnp.exp2(max_ref[slot] - top) * inverse
        weights = e_ref[slot] * part
        scores = (weights * (slope_ref[slot] - dot)).astype(HALF)
        spot = pl.ds(pl.multiple_of(slot * CHUNK, CHUNK), CHUNK)
        dv_acc[spot, :] += jnp.dot(weights.astype(HALF), g_ref[...], preferred_element_type=FULL)
        dk_acc[spot, :] += jnp.dot(scores, q_ref[...], preferred_element_type=FULL)
        dq_acc[...] += lax.dot_general(keys, scores, TN, preferred_element_type=FULL)

    def spot_of(index):
        return pl.ds(pl.multiple_of(index * CHUNK, CHUNK), CHUNK)

    state = (
        jnp.full((1, rows), -jnp.inf, FULL),
        jnp.zeros((1, rows), FULL),
        jnp.zeros((1, rows), FULL),
    )
    own = kv_refs[0]
    state = forward(tile_ref[0, spot_of(tile), :], own[1, spot_of(tile), :], tile, state, True)
    state = lax.fori_loop(
        0,
        tile,
        lambda i, s: forward(tile_ref[0, spot_of(i), :], own[1, spot_of(i), :], i, s, False),
        state,
    )
    for hop in range(1, HOPS + 1):
        ref = kv_refs[hop]
        state = lax.fori_loop(
            0,
            jnp.where(hop < hop_count, per_hop, 0),
            lambda i, s, ref=ref, hop=hop: forward(
                tile_ref[hop, spot_of(i), :],
                ref[1, spot_of(i), :],
                hop * per_hop + i,
                s,
                False,
            ),
            state,
        )
    top, total, dot = state
    inverse = 1.0 / total
    final = (top, inverse, dot * inverse)
    dq_acc[...] = jnp.zeros_like(dq_acc)
    for hop in range(HOPS + 1):
        trips = tile + 1 if hop == 0 else jnp.where(hop < hop_count, per_hop, 0)

        def step(i, carry, hop=hop):
            backward(tile_ref[hop, spot_of(i), :], hop * per_hop + i, final)
            return carry

        lax.fori_loop(0, trips, step, 0)
    dq_ref[...] = (dq_acc[...] * factor).T.astype(HALF)

    @pl.when(tile == tiles - 1)
    def _():
        dk_ref[...] = (dk_acc[...] * factor).astype(HALF)
        dv_ref[...] = dv_acc[...].astype(HALF)


def attention(g, hop_count, turn_parts, query_rows, grad_rows, own_pack, packs, groups, factor):
    total_rows, width = query_rows.shape
    length = own_pack.shape[2]
    tiles = length // CHUNK
    rows = total_rows // tiles
    hops = HOPS + 1
    keys = hops * length
    own_spec = pl.BlockSpec((2, None, length, width), lambda i: (0, g, 0, 0))
    hop_specs = [
        pl.BlockSpec((None, 2, None, length, width), lambda i, h=h: (h, 0, g, 0, 0))
        for h in range(HOPS)
    ]
    row_spec = pl.BlockSpec((rows, width), lambda i: (i, 0))
    part_spec = pl.BlockSpec((keys, width), lambda i: (0, 0))
    chunks = keys // CHUNK
    return pl.pallas_call(
        lambda *refs: attention_kernel(groups, factor, *refs),
        grid=(tiles,),
        in_specs=[
            pl.BlockSpec(memory_space=pltpu.SMEM),
            pl.BlockSpec(turn_parts.shape, lambda i: (0, 0, 0, 0)),
            row_spec,
            row_spec,
        ]
        + [own_spec]
        + hop_specs,
        out_specs=[row_spec, part_spec, part_spec],
        out_shape=[
            jax.ShapeDtypeStruct((total_rows, width), HALF),
            jax.ShapeDtypeStruct((keys, width), HALF),
            jax.ShapeDtypeStruct((keys, width), HALF),
        ],
        scratch_shapes=[
            pltpu.VMEM((chunks, CHUNK, rows), FULL),
            pltpu.VMEM((chunks, CHUNK, rows), FULL),
            pltpu.VMEM((chunks, 1, rows), FULL),
            pltpu.VMEM((keys, width), FULL),
            pltpu.VMEM((keys, width), FULL),
            pltpu.VMEM((width, rows), FULL),
            pltpu.VMEM((hops, length, width), HALF),
        ],
        compiler_params=pltpu.CompilerParams(vmem_limit_bytes=40 * 1024 * 1024),
        cost_estimate=pl.CostEstimate(
            flops=10 * total_rows * keys * width,
            bytes_accessed=6 * total_rows * width + 8 * keys * width,
            transcendentals=total_rows * keys,
        ),
    )(hop_count, turn_parts, query_rows, grad_rows, own_pack, *[packs] * HOPS)


def turn_sum_kernel(blocks, peers, terms_ref, out_ref, slots, send_sem, recv_sem):
    me, lane = lax.axis_index("ctx"), lax.axis_index("kv")
    pairs = [(j, z) for j in range(HOPS) for z in range(peers) if j or z]
    barrier = pltpu.get_barrier_semaphore()
    for j, z in pairs:
        source = (lax.rem(me - j + blocks, blocks), lax.rem(lane - z + peers, peers))
        pl.semaphore_signal(
            barrier, inc=1, device_id=source, device_id_type=pl.DeviceIdType.MESH
        )
    pl.semaphore_wait(barrier, len(pairs))
    copies = []
    for k, (j, z) in enumerate(pairs):
        copy = pltpu.make_async_remote_copy(
            src_ref=terms_ref.at[j],
            dst_ref=slots.at[k],
            send_sem=send_sem.at[k],
            recv_sem=recv_sem.at[k],
            device_id=(lax.rem(me + j, blocks), lax.rem(lane + z, peers)),
            device_id_type=pl.DeviceIdType.MESH,
        )
        copy.start()
        copies.append(copy)
    total = terms_ref[0].astype(FULL)
    for k, copy in enumerate(copies):
        copy.wait_recv()
        total = total + slots[k].astype(FULL)
    out_ref[...] = total
    for copy in copies:
        copy.wait_send()


def hand_on_kernel(blocks, pack_ref, turn_ref, pack_out, turn_out, next_out, send_sem, recv_sem):
    me, lane = lax.axis_index("ctx"), lax.axis_index("kv")
    shifts = list(range(1, HOPS + 1)) + [-h for h in range(1, HOPS)]
    barrier = pltpu.get_barrier_semaphore()
    for shift in shifts:
        pl.semaphore_signal(
            barrier,
            inc=1,
            device_id=(lax.rem(me - shift + blocks, blocks), lane),
            device_id_type=pl.DeviceIdType.MESH,
        )
    pl.semaphore_wait(barrier, len(shifts))
    jobs = [(turn_ref, turn_out.at[h - 1], h) for h in range(1, HOPS + 1)]
    jobs += [(turn_ref, next_out.at[h - 1], -h) for h in range(1, HOPS)]
    jobs += [(pack_ref, pack_out.at[h - 1], h) for h in range(1, HOPS + 1)]
    copies = []
    for k, (source, target, shift) in enumerate(jobs):
        copy = pltpu.make_async_remote_copy(
            src_ref=source,
            dst_ref=target,
            send_sem=send_sem.at[k],
            recv_sem=recv_sem.at[k],
            device_id=(lax.rem(me + shift + blocks, blocks), lane),
            device_id_type=pl.DeviceIdType.MESH,
        )
        copy.start()
        copies.append(copy)
    for copy in copies:
        copy.wait()


def hand_on(pack, turn):
    blocks = lax.axis_size("ctx")
    count = 3 * HOPS - 1
    hbm = pl.BlockSpec(memory_space=pl.ANY)
    return pl.pallas_call(
        lambda *refs: hand_on_kernel(blocks, *refs),
        out_shape=[
            jax.ShapeDtypeStruct((HOPS,) + pack.shape, HALF),
            jax.ShapeDtypeStruct((HOPS,) + turn.shape, FULL),
            jax.ShapeDtypeStruct((HOPS - 1,) + turn.shape, FULL),
        ],
        in_specs=[hbm, hbm],
        out_specs=[hbm] * 3,
        scratch_shapes=[
            pltpu.SemaphoreType.DMA((count,)),
            pltpu.SemaphoreType.DMA((count,)),
        ],
        compiler_params=pltpu.CompilerParams(collective_id=1, has_side_effects=True),
    )(pack, turn)


def turn_sum(terms):
    blocks, peers = lax.axis_size("ctx"), lax.axis_size("kv")
    count = HOPS * peers - 1
    return pl.pallas_call(
        lambda *refs: turn_sum_kernel(blocks, peers, *refs),
        out_shape=jax.ShapeDtypeStruct(terms.shape[1:], FULL),
        in_specs=[pl.BlockSpec(memory_space=pltpu.VMEM)],
        out_specs=pl.BlockSpec(memory_space=pltpu.VMEM),
        scratch_shapes=[
            pltpu.VMEM((count,) + terms.shape[1:], HALF),
            pltpu.SemaphoreType.DMA((count,)),
            pltpu.SemaphoreType.DMA((count,)),
        ],
        compiler_params=pltpu.CompilerParams(collective_id=0, has_side_effects=True),
    )(terms)


def shards(queries, key_heads, value_heads, grad_out, transforms, window, first_block):
    length, head_count, width = queries.shape
    kv_heads = key_heads.shape[1]
    groups = head_count // kv_heads
    factor = 1.0 / math.sqrt(width)
    blocks = lax.axis_size("ctx")
    position = (lax.axis_index("ctx") - first_block[0]) % blocks
    hop_counts = jnp.minimum(window, position + 1)
    own_pack = jnp.stack([key_heads.transpose(1, 0, 2), value_heads.transpose(1, 0, 2)])
    packs, arriving, later = hand_on(own_pack, transforms[0])
    met = [arriving[0]]
    for h in range(1, HOPS):
        met.append(jnp.dot(met[-1], arriving[h], precision=PRECISE))
    turn_parts = jnp.stack([jnp.stack(split_parts(m)) for m in met])
    turns = [transforms[0]] + [later[h - 1] for h in range(1, HOPS)]
    chain = [turns[0]]
    for h in range(1, HOPS - 1):
        chain.append(jnp.dot(turns[h], chain[-1], precision=PRECISE))
    own_keys = key_heads.transpose(1, 0, 2)
    query_rows = queries.reshape(length, kv_heads, groups, width).transpose(1, 0, 2, 3)
    grad_rows = grad_out.reshape(length, kv_heads, groups, width).transpose(1, 0, 2, 3)
    query_rows = query_rows.reshape(kv_heads, length * groups, width)
    grad_rows = grad_rows.reshape(kv_heads, length * groups, width)
    turned = [own_keys] + [times_split(own_keys, m, "gld,ed->gle").astype(HALF) for m in chain]
    query_parts, key_grads, value_grads = [], [], []
    turn_terms = [jnp.zeros((width, width), FULL) for _ in range(HOPS)]
    for g in range(kv_heads):
        dq, dk, dv = attention(
            g,
            hop_counts[g : g + 1],
            turn_parts,
            query_rows[g],
            grad_rows[g],
            own_pack,
            packs,
            groups,
            factor,
        )
        query_parts.append(dq)
        back = jnp.stack([dk, dv]).reshape(2, HOPS + 1, length, width)
        backs = [back[:, 0]] + [passed_along(back[:, h], -h) for h in range(1, HOPS + 1)]
        carried = backs[HOPS][0].astype(FULL)
        for h in range(HOPS, 0, -1):
            half = carried.astype(HALF)
            turn_terms[h - 1] += lax.dot_general(
                half, turned[h - 1][g], TN, preferred_element_type=FULL
            )
            carried = backs[h - 1][0].astype(FULL) + times_split(half, turns[h - 1], "le,ed->ld")
        key_grads.append(carried.astype(HALF))
        value_grads.append(sum(b[1].astype(FULL) for b in backs).astype(HALF))
    turn_total = turn_sum(jnp.stack(turn_terms).astype(HALF))
    query_grad = jnp.stack(query_parts).reshape(kv_heads, length, groups, width)
    query_grad = query_grad.transpose(1, 0, 2, 3).reshape(length, head_count, width)
    return (
        query_grad,
        jnp.stack(key_grads, axis=1),
        jnp.stack(value_grads, axis=1),
        turn_total[None],
    )


def solution(mesh):
    return jax.shard_map(
        shards,
        mesh=mesh,
        in_specs=(
            P("ctx", "kv", None),
            P("ctx", "kv", None),
            P("ctx", "kv", None),
            P("ctx", "kv", None),
            P("ctx", None, None),
            P("kv"),
            P(),
        ),
        out_specs=(
            P("ctx", "kv", None),
            P("ctx", "kv", None),
            P("ctx", "kv", None),
            P("ctx", None, None),
        ),
        check_vma=False,
    )
```

```python
import math

import jax
import jax.numpy as jnp
from jax import lax
from jax.experimental import pallas as pl
from jax.experimental.pallas import tpu as pltpu
from jax.sharding import PartitionSpec as P

HOPS = 3
CHUNK = 128
HALF = jnp.bfloat16
FULL = jnp.float32
PRECISE = lax.Precision.HIGHEST
NT = (((1,), (1,)), ((), ()))
TN = (((0,), (0,)), ((), ()))


def split_parts(matrix):
    upper = matrix.astype(HALF)
    lower = (matrix - upper.astype(FULL)).astype(HALF)
    return (upper, lower)


def times_split(rows_half, matrix, spec):
    upper, lower = split_parts(matrix)
    first = jnp.einsum(spec, rows_half, upper, preferred_element_type=FULL)
    return first + jnp.einsum(spec, rows_half, lower, preferred_element_type=FULL)


def attention_kernel(groups, factor, hops_ref, turn_ref, q_ref, g_ref, *refs):
    kv_refs = refs[: HOPS + 1]
    dq_ref, dk_ref, dv_ref, e_ref, slope_ref, max_ref, dk_acc, dv_acc, dq_acc, tile_ref = (
        refs[HOPS + 1 :]
    )
    tile = pl.program_id(0)
    tiles = pl.num_programs(0)
    rows = q_ref.shape[0]
    per_hop = kv_refs[0].shape[1] // CHUNK
    scale = factor * math.log2(math.e)
    hop_count = hops_ref[0]

    @pl.when(tile == 0)
    def _():
        dk_acc[...] = jnp.zeros_like(dk_acc)
        dv_acc[...] = jnp.zeros_like(dv_acc)
        tile_ref[0] = kv_refs[0][0]
        for hop in range(1, HOPS + 1):
            keys = kv_refs[hop][0]
            first = lax.dot_general(keys, turn_ref[hop - 1, 0], NT, preferred_element_type=FULL)
            second = lax.dot_general(keys, turn_ref[hop - 1, 1], NT, preferred_element_type=FULL)
            tile_ref[hop] = (first + second).astype(HALF)

    def forward(keys, values, slot, state, masked):
        top, total, dot = state
        logits = lax.dot_general(keys, q_ref[...], NT, preferred_element_type=FULL) * scale
        if masked:
            key_at = lax.broadcasted_iota(jnp.int32, (CHUNK, rows), 0)
            row_at = lax.broadcasted_iota(jnp.int32, (CHUNK, rows), 1) // groups
            logits = jnp.where(key_at <= row_at, logits, -jnp.inf)
        slopes = lax.dot_general(values, g_ref[...], NT, preferred_element_type=FULL)
        chunk_max = jnp.max(logits, axis=0, keepdims=True)
        exps = jnp.exp2(logits - chunk_max)
        e_ref[slot] = exps
        slope_ref[slot] = slopes
        max_ref[slot] = chunk_max
        top_new = jnp.maximum(top, chunk_max)
        old, new = jnp.exp2(top - top_new), jnp.exp2(chunk_max - top_new)
        total = total * old + jnp.sum(exps, axis=0, keepdims=True) * new
        dot = dot * old + jnp.sum(exps * slopes, axis=0, keepdims=True) * new
        return top_new, total, dot

    def backward(keys, slot, state):
        top, inverse, dot = state
        part = jnp.exp2(max_ref[slot] - top) * inverse
        weights = e_ref[slot] * part
        scores = (weights * (slope_ref[slot] - dot)).astype(HALF)
        spot = pl.ds(pl.multiple_of(slot * CHUNK, CHUNK), CHUNK)
        dv_acc[spot, :] += jnp.dot(weights.astype(HALF), g_ref[...], preferred_element_type=FULL)
        dk_acc[spot, :] += jnp.dot(scores, q_ref[...], preferred_element_type=FULL)
        dq_acc[...] += lax.dot_general(keys, scores, TN, preferred_element_type=FULL)

    def spot_of(index):
        return pl.ds(pl.multiple_of(index * CHUNK, CHUNK), CHUNK)

    state = (
        jnp.full((1, rows), -jnp.inf, FULL),
        jnp.zeros((1, rows), FULL),
        jnp.zeros((1, rows), FULL),
    )
    own = kv_refs[0]
    state = forward(tile_ref[0, spot_of(tile), :], own[1, spot_of(tile), :], tile, state, True)
    state = lax.fori_loop(
        0,
        tile,
        lambda i, s: forward(tile_ref[0, spot_of(i), :], own[1, spot_of(i), :], i, s, False),
        state,
    )
    for hop in range(1, HOPS + 1):
        ref = kv_refs[hop]
        state = lax.fori_loop(
            0,
            jnp.where(hop < hop_count, per_hop, 0),
            lambda i, s, ref=ref, hop=hop: forward(
                tile_ref[hop, spot_of(i), :],
                ref[1, spot_of(i), :],
                hop * per_hop + i,
                s,
                False,
            ),
            state,
        )
    top, total, dot = state
    inverse = 1.0 / total
    final = (top, inverse, dot * inverse)
    dq_acc[...] = jnp.zeros_like(dq_acc)
    for hop in range(HOPS + 1):
        trips = tile + 1 if hop == 0 else jnp.where(hop < hop_count, per_hop, 0)

        def step(i, carry, hop=hop):
            backward(tile_ref[hop, spot_of(i), :], hop * per_hop + i, final)
            return carry

        lax.fori_loop(0, trips, step, 0)
    dq_ref[...] = (dq_acc[...] * factor).T.astype(HALF)

    @pl.when(tile == tiles - 1)
    def _():
        dk_ref[...] = (dk_acc[...] * factor).astype(HALF)
        dv_ref[...] = dv_acc[...].astype(HALF)


def attention(g, hop_count, turn_parts, query_rows, grad_rows, own_pack, packs, groups, factor):
    total_rows, width = query_rows.shape
    length = own_pack.shape[2]
    tiles = length // CHUNK
    rows = total_rows // tiles
    hops = HOPS + 1
    keys = hops * length
    own_spec = pl.BlockSpec((2, None, length, width), lambda i: (0, g, 0, 0))
    hop_specs = [
        pl.BlockSpec((None, 2, None, length, width), lambda i, h=h: (h, 0, g, 0, 0))
        for h in range(HOPS)
    ]
    row_spec = pl.BlockSpec((rows, width), lambda i: (i, 0))
    part_spec = pl.BlockSpec((keys, width), lambda i: (0, 0))
    chunks = keys // CHUNK
    return pl.pallas_call(
        lambda *refs: attention_kernel(groups, factor, *refs),
        grid=(tiles,),
        in_specs=[
            pl.BlockSpec(memory_space=pltpu.SMEM),
            pl.BlockSpec(turn_parts.shape, lambda i: (0, 0, 0, 0)),
            row_spec,
            row_spec,
        ]
        + [own_spec]
        + hop_specs,
        out_specs=[row_spec, part_spec, part_spec],
        out_shape=[
            jax.ShapeDtypeStruct((total_rows, width), HALF),
            jax.ShapeDtypeStruct((keys, width), HALF),
            jax.ShapeDtypeStruct((keys, width), HALF),
        ],
        scratch_shapes=[
            pltpu.VMEM((chunks, CHUNK, rows), FULL),
            pltpu.VMEM((chunks, CHUNK, rows), FULL),
            pltpu.VMEM((chunks, 1, rows), FULL),
            pltpu.VMEM((keys, width), FULL),
            pltpu.VMEM((keys, width), FULL),
            pltpu.VMEM((width, rows), FULL),
            pltpu.VMEM((hops, length, width), HALF),
        ],
        compiler_params=pltpu.CompilerParams(vmem_limit_bytes=40 * 1024 * 1024),
        cost_estimate=pl.CostEstimate(
            flops=10 * total_rows * keys * width,
            bytes_accessed=6 * total_rows * width + 8 * keys * width,
            transcendentals=total_rows * keys,
        ),
    )(hop_count, turn_parts, query_rows, grad_rows, own_pack, *[packs] * HOPS)


def turn_sum_kernel(blocks, peers, terms_ref, out_ref, slots, send_sem, recv_sem):
    me, lane = lax.axis_index("ctx"), lax.axis_index("kv")
    pairs = [(j, z) for j in range(HOPS) for z in range(peers) if j or z]
    barrier = pltpu.get_barrier_semaphore()
    for j, z in pairs:
        source = (lax.rem(me - j + blocks, blocks), lax.rem(lane - z + peers, peers))
        pl.semaphore_signal(
            barrier, inc=1, device_id=source, device_id_type=pl.DeviceIdType.MESH
        )
    pl.semaphore_wait(barrier, len(pairs))
    copies = []
    for k, (j, z) in enumerate(pairs):
        copy = pltpu.make_async_remote_copy(
            src_ref=terms_ref.at[j],
            dst_ref=slots.at[k],
            send_sem=send_sem.at[k],
            recv_sem=recv_sem.at[k],
            device_id=(lax.rem(me + j, blocks), lax.rem(lane + z, peers)),
            device_id_type=pl.DeviceIdType.MESH,
        )
        copy.start()
        copies.append(copy)
    total = terms_ref[0].astype(FULL)
    for k, copy in enumerate(copies):
        copy.wait_recv()
        total = total + slots[k].astype(FULL)
    out_ref[...] = total
    for copy in copies:
        copy.wait_send()


def hand_on_kernel(blocks, pack_ref, turn_ref, pack_out, turn_out, next_out, send_sem, recv_sem):
    me, lane = lax.axis_index("ctx"), lax.axis_index("kv")
    shifts = list(range(1, HOPS + 1)) + [-h for h in range(1, HOPS)]
    barrier = pltpu.get_barrier_semaphore()
    for shift in shifts:
        pl.semaphore_signal(
            barrier,
            inc=1,
            device_id=(lax.rem(me - shift + blocks, blocks), lane),
            device_id_type=pl.DeviceIdType.MESH,
        )
    pl.semaphore_wait(barrier, len(shifts))
    jobs = [(turn_ref, turn_out.at[h - 1], h) for h in range(1, HOPS + 1)]
    jobs += [(turn_ref, next_out.at[h - 1], -h) for h in range(1, HOPS)]
    jobs += [(pack_ref, pack_out.at[h - 1], h) for h in range(1, HOPS + 1)]
    copies = []
    for k, (source, target, shift) in enumerate(jobs):
        copy = pltpu.make_async_remote_copy(
            src_ref=source,
            dst_ref=target,
            send_sem=send_sem.at[k],
            recv_sem=recv_sem.at[k],
            device_id=(lax.rem(me + shift + blocks, blocks), lane),
            device_id_type=pl.DeviceIdType.MESH,
        )
        copy.start()
        copies.append(copy)
    for copy in copies:
        copy.wait()


def hand_on(pack, turn):
    blocks = lax.axis_size("ctx")
    count = 3 * HOPS - 1
    hbm = pl.BlockSpec(memory_space=pl.ANY)
    return pl.pallas_call(
        lambda *refs: hand_on_kernel(blocks, *refs),
        out_shape=[
            jax.ShapeDtypeStruct((HOPS,) + pack.shape, HALF),
            jax.ShapeDtypeStruct((HOPS,) + turn.shape, FULL),
            jax.ShapeDtypeStruct((HOPS - 1,) + turn.shape, FULL),
        ],
        in_specs=[hbm, hbm],
        out_specs=[hbm] * 3,
        scratch_shapes=[
            pltpu.SemaphoreType.DMA((count,)),
            pltpu.SemaphoreType.DMA((count,)),
        ],
        compiler_params=pltpu.CompilerParams(collective_id=1, has_side_effects=True),
    )(pack, turn)


def hand_back_kernel(blocks, length, count, *refs):
    parts, (out_ref, send_sem, recv_sem) = refs[:count], refs[count:]
    me, lane = lax.axis_index("ctx"), lax.axis_index("kv")
    barrier = pltpu.get_barrier_semaphore()
    for h in range(1, HOPS + 1):
        pl.semaphore_signal(
            barrier,
            inc=1,
            device_id=(lax.rem(me + h, blocks), lane),
            device_id_type=pl.DeviceIdType.MESH,
        )
    pl.semaphore_wait(barrier, HOPS)
    copies = []
    for p in range(count):
        for h in range(1, HOPS + 1):
            k = p * HOPS + h - 1
            copy = pltpu.make_async_remote_copy(
                src_ref=parts[p].at[pl.ds(h * length, length)],
                dst_ref=out_ref.at[h - 1, p],
                send_sem=send_sem.at[k],
                recv_sem=recv_sem.at[k],
                device_id=(lax.rem(me - h + blocks, blocks), lane),
                device_id_type=pl.DeviceIdType.MESH,
            )
            copy.start()
            copies.append(copy)
    for copy in copies:
        copy.wait()


def hand_back(parts, length):
    blocks = lax.axis_size("ctx")
    count = len(parts)
    hbm = pl.BlockSpec(memory_space=pl.ANY)
    return pl.pallas_call(
        lambda *refs: hand_back_kernel(blocks, length, count, *refs),
        out_shape=jax.ShapeDtypeStruct((HOPS, count, length, parts[0].shape[1]), HALF),
        in_specs=[hbm] * count,
        out_specs=hbm,
        scratch_shapes=[
            pltpu.SemaphoreType.DMA((count * HOPS,)),
            pltpu.SemaphoreType.DMA((count * HOPS,)),
        ],
        compiler_params=pltpu.CompilerParams(collective_id=2, has_side_effects=True),
    )(*parts)


def turn_sum(terms):
    blocks, peers = lax.axis_size("ctx"), lax.axis_size("kv")
    count = HOPS * peers - 1
    return pl.pallas_call(
        lambda *refs: turn_sum_kernel(blocks, peers, *refs),
        out_shape=jax.ShapeDtypeStruct(terms.shape[1:], FULL),
        in_specs=[pl.BlockSpec(memory_space=pltpu.VMEM)],
        out_specs=pl.BlockSpec(memory_space=pltpu.VMEM),
        scratch_shapes=[
            pltpu.VMEM((count,) + terms.shape[1:], HALF),
            pltpu.SemaphoreType.DMA((count,)),
            pltpu.SemaphoreType.DMA((count,)),
        ],
        compiler_params=pltpu.CompilerParams(collective_id=0, has_side_effects=True),
    )(terms)


def shards(queries, key_heads, value_heads, grad_out, transforms, window, first_block):
    length, head_count, width = queries.shape
    kv_heads = key_heads.shape[1]
    groups = head_count // kv_heads
    factor = 1.0 / math.sqrt(width)
    blocks = lax.axis_size("ctx")
    position = (lax.axis_index("ctx") - first_block[0]) % blocks
    hop_counts = jnp.minimum(window, position + 1)
    own_pack = jnp.stack([key_heads.transpose(1, 0, 2), value_heads.transpose(1, 0, 2)])
    packs, arriving, later = hand_on(own_pack, transforms[0])
    met = [arriving[0]]
    for h in range(1, HOPS):
        met.append(jnp.dot(met[-1], arriving[h], precision=PRECISE))
    turn_parts = jnp.stack([jnp.stack(split_parts(m)) for m in met])
    turns = [transforms[0]] + [later[h - 1] for h in range(1, HOPS)]
    chain = [turns[0]]
    for h in range(1, HOPS - 1):
        chain.append(jnp.dot(turns[h], chain[-1], precision=PRECISE))
    own_keys = key_heads.transpose(1, 0, 2)
    query_rows = queries.reshape(length, kv_heads, groups, width).transpose(1, 0, 2, 3)
    grad_rows = grad_out.reshape(length, kv_heads, groups, width).transpose(1, 0, 2, 3)
    query_rows = query_rows.reshape(kv_heads, length * groups, width)
    grad_rows = grad_rows.reshape(kv_heads, length * groups, width)
    turned = [own_keys] + [times_split(own_keys, m, "gld,ed->gle").astype(HALF) for m in chain]
    query_parts, key_grads, value_grads, parts = [], [], [], []
    turn_terms = [jnp.zeros((width, width), FULL) for _ in range(HOPS)]
    for g in range(kv_heads):
        dq, dk, dv = attention(
            g,
            hop_counts[g : g + 1],
            turn_parts,
            query_rows[g],
            grad_rows[g],
            own_pack,
            packs,
            groups,
            factor,
        )
        query_parts.append(dq)
        parts += [dk, dv]
    landed = hand_back(parts, length)
    for g in range(kv_heads):
        backs = [(parts[2 * g][:length], parts[2 * g + 1][:length])]
        backs += [(landed[h, 2 * g], landed[h, 2 * g + 1]) for h in range(HOPS)]
        carried = backs[HOPS][0].astype(FULL)
        for h in range(HOPS, 0, -1):
            half = carried.astype(HALF)
            turn_terms[h - 1] += lax.dot_general(
                half, turned[h - 1][g], TN, preferred_element_type=FULL
            )
            carried = backs[h - 1][0].astype(FULL) + times_split(half, turns[h - 1], "le,ed->ld")
        key_grads.append(carried.astype(HALF))
        value_grads.append(sum(b[1].astype(FULL) for b in backs).astype(HALF))
    turn_total = turn_sum(jnp.stack(turn_terms).astype(HALF))
    query_grad = jnp.stack(query_parts).reshape(kv_heads, length, groups, width)
    query_grad = query_grad.transpose(1, 0, 2, 3).reshape(length, head_count, width)
    return (
        query_grad,
        jnp.stack(key_grads, axis=1),
        jnp.stack(value_grads, axis=1),
        turn_total[None],
    )


def solution(mesh):
    return jax.shard_map(
        shards,
        mesh=mesh,
        in_specs=(
            P("ctx", "kv", None),
            P("ctx", "kv", None),
            P("ctx", "kv", None),
            P("ctx", "kv", None),
            P("ctx", None, None),
            P("kv"),
            P(),
        ),
        out_specs=(
            P("ctx", "kv", None),
            P("ctx", "kv", None),
            P("ctx", "kv", None),
            P("ctx", None, None),
        ),
        check_vma=False,
    )
```
